256 devices in a mesh: chan: 64 (over x, y_hi, z), freq: 4 (over y_lo, core).
Axes of the slice: x: 4, y: 4 (y_hi: 2, y_lo: 2; y = y_hi * 2 + y_lo), z: 8, core: 2. Of those that a mesh axis runs over, the one named last changes fastest.
Arguments:
- spectra: bfloat16 [2, 2048, 64, 512], P(None, 'chan', None, 'freq'), may hold values from -600 to 600
- offsets: int32 [3], replicated, may hold values from 1 to 32, as said below
- alive: int32 [2048], P('chan'), may hold values 0 or 1
Outputs:
- pair_corr: float32 [3, 2048, 32, 384], P(None, ('chan', 'freq'))
The draws below stay inside these ranges and needn't reach their ends.
Inputs may be any that keep to these rules, and one draw needn't show every extreme that they name: The offsets are distinct; one of them is 1 and one is 32.
All inputs are finite; a program needn't handle non-finite values. No bound on the sum of `alive` on one device may be relied on, other than what follows from the above.
Results may differ from the reference program's by a relative error of at most 0.0041.
Values may be sent and summed in bfloat16 or wider, within the bound.
No kernel may reach another device: no remote copies, remote signals or barrier semaphores. Data moves between devices by JAX's collectives and lax.ppermute only.
A program may use at most 384 MiB of HBM per device.

```python
import math
import jax
import jax.numpy as jnp
from jax import lax

CH_DEV = 32
W = 64
F = 512
BAND = 128
HALF_LAG = 192
ROUNDS = 3
BLOCKS = 64
CHANNELS = 2048
LAGS = 384


def draw_spectra(key, part):
    key = jax.random.fold_in(key, 11)
    key_base, key_rows, key_bins = jax.random.split(key, 3)
    base = jnp.clip(jax.random.normal(key_base, (2, CHANNELS, W, F), jnp.float32), -6.0, 6.0)
    row_top = 10.0
    row_scale = jnp.exp(jax.random.uniform(key_rows, (1, CHANNELS, W, 1), jnp.float32) * jnp.log(row_top))
    bin_scale = jnp.exp(jax.random.uniform(key_bins, (1, CHANNELS, 1, F), jnp.float32) * jnp.log(10.0))
    return jnp.clip(base * row_scale * bin_scale, -600.0, 600.0).astype(jnp.bfloat16)


def draw_offsets(key, part):
    key = jax.random.fold_in(key, 23)
    key_pick, key_order = jax.random.split(key, 2)
    middle = jax.random.permutation(key_pick, BLOCKS // 2 - 2)[:ROUNDS - 2] + 2
    chosen = jnp.concatenate([jnp.array([1, BLOCKS // 2], jnp.int32), middle.astype(jnp.int32)])
    return jax.random.permutation(key_order, chosen).astype(jnp.int32)


def plant(result, own_key, low, largest):
    dims = result.shape
    spot = [jax.random.randint(jax.random.fold_in(own_key, axis), (), 0, dims[axis]) for axis in range(len(dims))]
    result = result.at[tuple(spot)].set(low)
    longest = dims.index(max(dims))
    spot[longest] = (spot[longest] + 1) % dims[longest]
    return result.at[tuple(spot)].set(largest)


def setup_inputs(seed: int = 0) -> dict:
    keys = jax.random.split(jax.random.key(seed), 4)
    return {
        "spectra": draw_spectra(jax.random.fold_in(keys[3], 71), 0),
        "offsets": draw_offsets(jax.random.fold_in(keys[3], 71), 0),
        "alive": plant((jax.random.randint(keys[2], (CHANNELS,), 0, 8) < 7).astype(jnp.int32), jax.random.fold_in(keys[2], 1), 0, 1),
    }


EPS = 1e-06

def whiten(spectra, alive):
    values = spectra.astype(jnp.float32)
    energy = values[0] * values[0] + values[1] * values[1]
    chan_count = energy.shape[0]
    window_count = energy.shape[1]
    bin_count = energy.shape[2]
    banded = lax.optimization_barrier(jnp.mean(energy.reshape(chan_count, window_count, bin_count // BAND, BAND), axis=3))
    amplitude = jnp.sqrt(banded + EPS)
    shaped = values.reshape(2, chan_count, window_count, bin_count // BAND, BAND)
    scaled = shaped / amplitude[None, :, :, :, None] * alive.astype(jnp.float32)[None, :, None, None, None]
    return scaled.reshape(2, chan_count, window_count, bin_count).astype(jnp.bfloat16)

def lag_table(first_bin, count):
    bin_index = first_bin + jnp.arange(count, dtype=jnp.int32)
    lag_index = jnp.arange(LAGS, dtype=jnp.int32) - HALF_LAG
    phase = jnp.mod(bin_index[:, None] * lag_index[None, :], 2 * F)
    angle = math.pi / F * phase.astype(jnp.float32)
    factor = 1.0 / math.sqrt(W * F)
    return jnp.concatenate([jnp.cos(angle), -jnp.sin(angle)], axis=0) * factor

def reference(spectra, offsets, alive):
    whitened = whiten(spectra, alive)
    blocks = whitened.reshape(2, BLOCKS, CH_DEV, W, F)
    rotated = jnp.stack([blocks, jnp.stack([blocks[1], -blocks[0]])])
    table = lag_table(0, F)

    def one_block(pair):
        own, other = pair
        cross = jnp.einsum('jkcwf,kdwf->cdjf', own.astype(jnp.float32), other.astype(jnp.float32), precision=lax.Precision.HIGHEST)
        flat = cross.reshape(CH_DEV * CH_DEV, 2 * F)
        return jnp.dot(flat, table, precision=lax.Precision.HIGHEST).reshape(CH_DEV, CH_DEV, LAGS)
    results = []
    for which_round in range(ROUNDS):
        partner = jnp.roll(blocks, offsets[which_round], axis=1)
        per_block = lax.map(one_block, (jnp.moveaxis(rotated, 2, 0), jnp.moveaxis(partner, 1, 0)))
        results.append(per_block.reshape(CHANNELS, CH_DEV, LAGS))
    return jnp.stack(results)
```

```python
import functools
import math

import jax
import jax.numpy as jnp
import numpy as np
from jax import lax
from jax.experimental import pallas as pl
from jax.experimental.pallas import tpu as pltpu
from jax.sharding import PartitionSpec as P

W = 64
F = 512
HALF_LAG = 192
LAGS = 384
CH = 32
BINS = 128
KW = 2 * W
GROUPS = 4
OWN = CH // GROUPS
QUAD = 4
EPS = 1e-06
VMEM_LIMIT = 48 * 1024 * 1024


def whole(shape_rank):
    return pl.BlockSpec(memory_space=pltpu.VMEM)


def whiten_kernel(alive_ref, x_ref, out_ref, turned):
    def one_channel(c, carry):
        re = x_ref[0, c].astype(jnp.float32)
        im = x_ref[1, c].astype(jnp.float32)
        energy = jnp.mean(re * re + im * im, axis=1, keepdims=True)
        scale = alive_ref[c].astype(jnp.float32) / jnp.sqrt(energy + EPS)
        both = jnp.concatenate([re * scale, im * scale], axis=0)
        turned[pl.ds(pl.multiple_of(c * BINS, BINS), BINS), :] = both.T
        return carry

    lax.fori_loop(0, CH, one_channel, 0, unroll=4)

    def one_bin(f, carry):
        rows = turned[pl.ds(f, CH, stride=BINS), :]
        out_ref[f] = rows.astype(jnp.bfloat16)
        return carry

    lax.fori_loop(0, BINS, one_bin, 0, unroll=8)


def whiten(spectra, alive):
    return pl.pallas_call(
        whiten_kernel,
        out_shape=jax.ShapeDtypeStruct((BINS, CH, KW), jnp.bfloat16),
        in_specs=[pl.BlockSpec(memory_space=pltpu.SMEM), pl.BlockSpec(memory_space=pltpu.VMEM)],
        out_specs=pl.BlockSpec(memory_space=pltpu.VMEM),
        scratch_shapes=[pltpu.VMEM((CH * BINS, KW), jnp.float32)],
        compiler_params=pltpu.CompilerParams(vmem_limit_bytes=VMEM_LIMIT),
        cost_estimate=pl.CostEstimate(flops=4_000_000, bytes_accessed=2 << 20, transcendentals=2048),
    )(alive, spectra)


def rotate_kernel(own_ref, out_ref):
    lane = lax.broadcasted_iota(jnp.int32, (CH, KW), 1)

    def one_bin(f, carry):
        rows = own_ref[f]
        out_ref[f, 0:CH, :] = rows
        other = pltpu.roll(rows.astype(jnp.float32), W, 1)
        out_ref[f, CH : 2 * CH, :] = jnp.where(lane < W, other, -other).astype(jnp.bfloat16)
        return carry

    lax.fori_loop(0, BINS, one_bin, 0, unroll=8)


def rotate(own):
    return pl.pallas_call(
        rotate_kernel,
        out_shape=jax.ShapeDtypeStruct((BINS, 2 * CH, KW), jnp.bfloat16),
        in_specs=[pl.BlockSpec(memory_space=pltpu.VMEM)],
        out_specs=pl.BlockSpec(memory_space=pltpu.VMEM),
        compiler_params=pltpu.CompilerParams(vmem_limit_bytes=VMEM_LIMIT),
        cost_estimate=pl.CostEstimate(flops=4_000_000, bytes_accessed=3 << 20, transcendentals=0),
    )(own)


def cross_kernel(place_ref, own_ref, partner_ref, *rest):
    outs, scratch = rest[:GROUPS], rest[GROUPS]
    place = place_ref[0]

    def one_bin(f, carry):
        scratch[pl.ds(pl.multiple_of(f * 2 * CH, 2 * CH), 2 * CH), 0:CH] = lax.dot_general(
            own_ref[f], partner_ref[f], (((1,), (1,)), ((), ())), preferred_element_type=jnp.float32
        )
        return carry

    lax.fori_loop(0, BINS, one_bin, 0, unroll=8)
    lane = lax.broadcasted_iota(jnp.int32, (BINS, KW), 1)
    for s in range(GROUPS):
        group = lax.rem(place + s, GROUPS)
        for j in range(2):
            for quad in range(OWN // QUAD):
                packed = None
                for i in range(QUAD):
                    row = j * CH + group * OWN + quad * QUAD + i
                    piece = scratch[pl.ds(row, BINS, stride=2 * CH), :]
                    if i:
                        piece = pltpu.roll(piece, CH * i, 1)
                        packed = jnp.where(lane >= CH * i, piece, packed)
                    else:
                        packed = piece
                outs[s][j, quad] = packed.astype(jnp.bfloat16)


def cross(place, own, partner):
    part = jax.ShapeDtypeStruct((2, OWN // QUAD, BINS, QUAD * CH), jnp.bfloat16)
    return pl.pallas_call(
        cross_kernel,
        out_shape=[part] * GROUPS,
        in_specs=[pl.BlockSpec(memory_space=pltpu.SMEM)] + [pl.BlockSpec(memory_space=pltpu.VMEM)] * 2,
        out_specs=[pl.BlockSpec(memory_space=pltpu.VMEM)] * GROUPS,
        scratch_shapes=[pltpu.VMEM((BINS * 2 * CH, KW), jnp.float32)],
        compiler_params=pltpu.CompilerParams(vmem_limit_bytes=VMEM_LIMIT),
        cost_estimate=pl.CostEstimate(flops=67_000_000, bytes_accessed=4 << 20, transcendentals=0),
    )(place, own, partner)


def lag_tables():
    bins = np.arange(F)[:, None]
    lags = np.arange(LAGS)[None, :] - HALF_LAG
    angle = np.mod(bins * lags, 2 * F) * (math.pi / F)
    factor = 1.0 / math.sqrt(W * F)
    table = np.stack([np.cos(angle), -np.sin(angle)]) * factor
    table = table.reshape(2, GROUPS, BINS, LAGS).transpose(1, 3, 0, 2).reshape(GROUPS, LAGS, 2 * BINS)
    high = table.astype(jnp.bfloat16)
    low = (table - high.astype(np.float64)).astype(jnp.bfloat16)
    return high, low


def lags_kernel(offsets_ref, place_ref, high_ref, low_ref, *rest):
    parts, out_ref = rest[:-1], rest[-1]
    place = place_ref[0]
    item = pl.program_id(0)

    def one_item(blocks):
        for quad in range(OWN // QUAD):
            total = jnp.zeros((LAGS, QUAD * CH), jnp.float32)
            for s in range(GROUPS):
                source = lax.rem(place + GROUPS - s, GROUPS)
                terms = blocks[s][:, quad].reshape(2 * BINS, QUAD * CH)
                total += jnp.dot(high_ref[source], terms, preferred_element_type=jnp.float32)
                total += jnp.dot(low_ref[source], terms, preferred_element_type=jnp.float32)
            out_ref[0, quad * QUAD * CH : (quad + 1) * QUAD * CH, :] = total.T

    for k in range(len(parts) // GROUPS):
        pl.when(item == k)(functools.partial(one_item, parts[k * GROUPS : (k + 1) * GROUPS]))


def lags(offsets, place, parts):
    rounds = len(parts) // GROUPS

    def block_of(item, offsets_ref, place_ref):
        one = jnp.where(offsets_ref[0] == 1, 0, jnp.where(offsets_ref[1] == 1, 1, 2))
        far = jnp.where(offsets_ref[0] == 32, 0, jnp.where(offsets_ref[1] == 32, 1, 2))
        return jnp.where(item == 0, one, jnp.where(item == 1, far, 3 - one - far)), 0, 0

    high, low = lag_tables()
    return pl.pallas_call(
        lags_kernel,
        out_shape=jax.ShapeDtypeStruct((rounds, OWN * CH, LAGS), jnp.float32),
        grid_spec=pltpu.PrefetchScalarGridSpec(
            num_scalar_prefetch=2,
            grid=(rounds,),
            in_specs=[pl.BlockSpec(memory_space=pltpu.VMEM)] * (2 + len(parts)),
            out_specs=pl.BlockSpec((1, OWN * CH, LAGS), block_of),
        ),
        compiler_params=pltpu.CompilerParams(vmem_limit_bytes=VMEM_LIMIT),
        cost_estimate=pl.CostEstimate(flops=1_200_000_000, bytes_accessed=4 << 20, transcendentals=0),
    )(offsets, place, jnp.asarray(high), jnp.asarray(low), *parts)


def from_behind(block, axis, distance):
    size = lax.axis_size(axis)
    return lax.ppermute(block, axis, [((i - distance) % size, i) for i in range(size)])


def spread(blocks):
    return [blocks[0]] + [from_behind(blocks[s], "freq", s) for s in range(1, GROUPS)]


def local(spectra, offsets, alive):
    half = lax.axis_size("chan") // 2
    place = lax.axis_index("freq").astype(jnp.int32).reshape(1)
    own = whiten(spectra, alive)
    next_one = from_behind(own, "chan", 1)
    far_one = from_behind(own, "chan", half)
    branches = [functools.partial(from_behind, axis="chan", distance=k) for k in range(2, half)]
    other = lax.switch(jnp.sum(offsets) - (1 + half + 2), branches, own)
    both = rotate(own)
    parts = []
    for partner in (next_one, far_one, other):
        parts += spread(cross(place, both, partner))
    result = lags(offsets, place, parts)
    return result.reshape(3, OWN, CH, LAGS)


def solution(mesh):
    return jax.shard_map(
        local,
        mesh=mesh,
        in_specs=(P(None, "chan", None, "freq"), P(), P("chan")),
        out_specs=P(None, ("chan", "freq"), None, None),
        check_vma=False,
    )
```

```python
import functools
import math

import jax
import jax.numpy as jnp
import numpy as np
from jax import lax
from jax.experimental import pallas as pl
from jax.experimental.pallas import tpu as pltpu
from jax.sharding import PartitionSpec as P

W = 64
F = 512
HALF_LAG = 192
LAGS = 384
CH = 32
BINS = 128
KW = 2 * W
GROUPS = 4
OWN = CH // GROUPS
QUAD = 4
EPS = 1e-06
STEP = BINS + 8
PITCH = 2 * CH + 8
BLOCKS_Z = 8
SMALL = pl.CostEstimate(flops=1, bytes_accessed=1, transcendentals=0)


def whiten_kernel(offsets_ref, alive_ref, x_ref, out_ref, rest_ref, turned):
    rest_ref[0] = offsets_ref[0] + offsets_ref[1] + offsets_ref[2]

    def one_channel(c, carry):
        re = x_ref[0, c].astype(jnp.float32)
        im = x_ref[1, c].astype(jnp.float32)
        energy = jnp.mean(re * re + im * im, axis=1, keepdims=True)
        scale = alive_ref[c].astype(jnp.float32) / jnp.sqrt(energy + EPS)
        both = jnp.concatenate([re * scale, im * scale], axis=0)
        turned[pl.ds(pl.multiple_of(c * STEP, 8), BINS), :] = both.T
        return carry

    lax.fori_loop(0, CH, one_channel, 0, unroll=8)

    def one_bin(f, carry):
        rows = turned[pl.ds(f, CH, stride=STEP), :]
        out_ref[f] = rows.astype(jnp.bfloat16)
        return carry

    lax.fori_loop(0, BINS, one_bin, 0, unroll=16)


def whiten(spectra, offsets, alive):
    return pl.pallas_call(
        whiten_kernel,
        out_shape=[jax.ShapeDtypeStruct((BINS, CH, KW), jnp.bfloat16), jax.ShapeDtypeStruct((1,), jnp.int32)],
        in_specs=[pl.BlockSpec(memory_space=pltpu.SMEM)] * 2 + [pl.BlockSpec(memory_space=pltpu.VMEM)],
        out_specs=[pl.BlockSpec(memory_space=pltpu.VMEM), pl.BlockSpec(memory_space=pltpu.SMEM)],
        scratch_shapes=[pltpu.VMEM((CH * STEP, KW), jnp.float32)],
        compiler_params=pltpu.CompilerParams(vmem_limit_bytes=62 << 20),
        cost_estimate=SMALL,
    )(offsets, alive, spectra)


def rotate_kernel(own_ref, out_ref):
    lane = lax.broadcasted_iota(jnp.int32, (CH, KW), 1)

    def one_bin(f, carry):
        rows = own_ref[f]
        out_ref[f, 0:CH, :] = rows
        other = pltpu.roll(rows.astype(jnp.float32), W, 1)
        out_ref[f, CH : 2 * CH, :] = jnp.where(lane < W, other, -other).astype(jnp.bfloat16)
        return carry

    lax.fori_loop(0, BINS, one_bin, 0, unroll=8)


def rotate(own):
    return pl.pallas_call(
        rotate_kernel,
        out_shape=jax.ShapeDtypeStruct((BINS, 2 * CH, KW), jnp.bfloat16),
        in_specs=[pl.BlockSpec(memory_space=pltpu.VMEM)],
        out_specs=pl.BlockSpec(memory_space=pltpu.VMEM),
        compiler_params=pltpu.CompilerParams(vmem_limit_bytes=24 << 20),
        cost_estimate=SMALL,
    )(own)


def cross_kernel(layout, place_ref, own_ref, *rest):
    pieces, outs, scratch = rest[: len(rest) - 1 - len(layout)], rest[len(rest) - 1 - len(layout) : -1], rest[-1]
    group_refs = {}
    for out_ref, held in zip(outs, layout):
        for n, k in enumerate(held):
            group_refs[k] = out_ref.at[n]
    place = place_ref[0]
    first = 0
    for piece_ref in pieces:
        bins = piece_ref.shape[0]

        def one_bin(f, carry, first=first, piece_ref=piece_ref):
            here = pl.multiple_of((first + f) * PITCH, 8)
            scratch[pl.ds(here, 2 * CH), 0:CH] = lax.dot_general(
                own_ref[first + f], piece_ref[f], (((1,), (1,)), ((), ())), preferred_element_type=jnp.float32
            )
            return carry

        lax.fori_loop(0, bins, one_bin, 0, unroll=max(n for n in range(1, 33) if bins % n == 0))
        first += bins
    lane = lax.broadcasted_iota(jnp.int32, (BINS, KW), 1)
    for k in range(GROUPS):
        group = lax.bitwise_xor(place, k)

        def one_part(j, carry, k=k, group=group):
            for quad in range(OWN // QUAD):
                row = j * CH + group * OWN + quad * QUAD
                packed = scratch[pl.ds(row, BINS, stride=PITCH), :]
                for i in range(1, QUAD):
                    piece = scratch[pl.ds(row + i, BINS, stride=PITCH), :]
                    packed = jnp.where(lane >= CH * i, pltpu.roll(piece, CH * i, 1), packed)
                here = pl.ds(pl.multiple_of(j * BINS, BINS), BINS)
                group_refs[k][here, quad * QUAD * CH : (quad + 1) * QUAD * CH] = packed.astype(jnp.bfloat16)
            return carry

        lax.fori_loop(0, 2, one_part, 0)


def cross(place, own, pieces, layout):
    outs = [jax.ShapeDtypeStruct((len(held), 2 * BINS, OWN * CH), jnp.bfloat16) for held in layout]
    return pl.pallas_call(
        functools.partial(cross_kernel, layout),
        out_shape=outs,
        in_specs=[pl.BlockSpec(memory_space=pltpu.SMEM)] + [pl.BlockSpec(memory_space=pltpu.VMEM)] * (1 + len(pieces)),
        out_specs=[pl.BlockSpec(memory_space=pltpu.VMEM)] * len(outs),
        scratch_shapes=[pltpu.VMEM((BINS * PITCH, KW), jnp.float32)],
        compiler_params=pltpu.CompilerParams(vmem_limit_bytes=24 << 20),
        cost_estimate=SMALL,
    )(place, own, *pieces)


@functools.cache
def lag_tables():
    bins = np.arange(F)[:, None]
    lags = np.arange(LAGS)[None, :] - HALF_LAG
    angle = np.mod(bins * lags, 2 * F) * (math.pi / F)
    factor = 1.0 / math.sqrt(W * F)
    table = np.stack([np.cos(angle), -np.sin(angle)]) * factor
    table = table.reshape(2, GROUPS, BINS, LAGS).transpose(1, 3, 0, 2).reshape(GROUPS, LAGS, 2 * BINS)
    high = table.astype(jnp.bfloat16)
    low = (table - high.astype(np.float64)).astype(jnp.bfloat16)
    return high, low


def lags_kernel(counts, offsets_ref, place_ref, high_ref, low_ref, *rest):
    out_ref = rest[-1]
    place = place_ref[0]

    def one_item(parts):
        blocks = [part.at[n] for part in parts for n in range(part.shape[0])]
        total = jnp.zeros((LAGS, OWN * CH), jnp.float32)
        for k in range(GROUPS):
            source = lax.bitwise_xor(place, k)
            terms = blocks[k][...]
            total += jnp.dot(high_ref[source], terms, preferred_element_type=jnp.float32)
            total += jnp.dot(low_ref[source], terms, preferred_element_type=jnp.float32)
        out_ref[0] = total.T

    first = 0
    for item, count in enumerate(counts):
        pl.when(pl.program_id(0) == item)(functools.partial(one_item, rest[first : first + count]))
        first += count


def lags(offsets, place, items):
    def block_of(step, offsets_ref, place_ref):
        one = jnp.where(offsets_ref[0] == 1, 0, jnp.where(offsets_ref[1] == 1, 1, 2))
        far = jnp.where(offsets_ref[0] == 32, 0, jnp.where(offsets_ref[1] == 32, 1, 2))
        return jnp.where(step == 0, one, jnp.where(step == 1, far, 3 - one - far)), 0, 0

    counts = [len(parts) for parts in items]
    return pl.pallas_call(
        functools.partial(lags_kernel, counts),
        out_shape=jax.ShapeDtypeStruct((len(items), OWN * CH, LAGS), jnp.float32),
        grid_spec=pltpu.PrefetchScalarGridSpec(
            num_scalar_prefetch=2,
            grid=(len(items),),
            in_specs=[pl.BlockSpec(memory_space=pltpu.VMEM)] * (2 + sum(counts)),
            out_specs=pl.BlockSpec((1, OWN * CH, LAGS), block_of),
        ),
        compiler_params=pltpu.CompilerParams(vmem_limit_bytes=24 << 20),
        cost_estimate=SMALL,
    )(offsets, place, *[jnp.asarray(t) for t in lag_tables()], *[part for parts in items for part in parts])


def swap(block, k):
    return lax.ppermute(block, "freq", [(i, i ^ k) for i in range(GROUPS)])


def walk(block, before, after, takes_part=lambda b: True):
    count = lax.axis_size("chan")
    route = [(before(b) % count, after(b) % count) for b in range(count) if takes_part(b)]
    return lax.ppermute(block, "chan", route)


def home(b):
    return b


def ahead(distance):
    return lambda b: b + distance


def along_z(places):
    return lambda b: b // BLOCKS_Z * BLOCKS_Z + (b + places) % BLOCKS_Z


STRAIGHT, FROM_NEXT, ALONG_Z = range(3)
PIECES = [
    [(128, STRAIGHT, 0)],
    [(128, FROM_NEXT, 0)],
    [(128, FROM_NEXT, 0)],
    [(72, FROM_NEXT, 0), (56, ALONG_Z, -3)],
    [(72, FROM_NEXT, 0), (56, ALONG_Z, -2)],
    [(32, ALONG_Z, 2), (96, STRAIGHT, 0)],
    [(128, STRAIGHT, 0)],
    [(128, STRAIGHT, 0)],
]


def with_other_at(distance, offsets, place, own):
    half = lax.axis_size("chan") // 2
    goal = ahead(distance)
    back = ahead(-2 * BLOCKS_Z)
    plan, cuts, low = PIECES[distance % BLOCKS_Z], [], 0
    for bins, how, places in plan:
        cuts.append(own[low : low + bins])
        low += bins
    both_ways = distance >= 2 * BLOCKS_Z
    cut = 80 if both_ways else BINS // 2
    own, cuts, split = lax.optimization_barrier((own, cuts, (own[:cut], own[cut:])))

    stopped = [
        walk(piece, home, along_z(places)) if how == ALONG_Z else None for piece, (_, how, places) in zip(cuts, plan)
    ]
    next_one = walk(own, home, ahead(1))
    next_one, both = lax.optimization_barrier((next_one, rotate(own)))
    far_ones = [walk(walk(piece, home, back), back, ahead(half)) for piece in split[int(both_ways) :]]
    if both_ways:
        far_ones.insert(0, walk(split[0], home, ahead(half)))
    pieces, low = [], 0
    for piece, stop, (bins, how, places) in zip(cuts, stopped, plan):
        if how == STRAIGHT:
            pieces.append(walk(piece, home, goal))
        elif how == ALONG_Z:
            pieces.append(walk(stop, along_z(places), goal))
        else:
            pieces.append(walk(next_one[low : low + bins], ahead(1), goal))
        low += bins

    layout = [(k,) for k in range(GROUPS)]

    def spread(groups):
        return [groups[0]] + [swap(groups[k], k) for k in (1, 2, 3)]

    near = spread(cross(place, both, [next_one], layout))
    far = cross(place, both, far_ones, layout)
    early = all(how != STRAIGHT for _, how, _ in plan)
    if early:
        far = spread(far)
    pieces, near, far = lax.optimization_barrier((pieces, near, far))
    if not early:
        far = spread(far)
    other = spread(cross(place, both, pieces, layout))
    return lags(offsets, place, [near, far, other])


def local(spectra, offsets, alive):
    half = lax.axis_size("chan") // 2
    place = lax.axis_index("freq").astype(jnp.int32).reshape(1)
    own, total = whiten(spectra, offsets, alive)
    branches = [functools.partial(with_other_at, distance) for distance in range(2, half)]
    result = lax.switch(total[0] - (1 + half + 2), branches, offsets, place, own)
    return result.reshape(3, OWN, CH, LAGS)


def solution(mesh):
    return jax.shard_map(
        local,
        mesh=mesh,
        in_specs=(P(None, "chan", None, "freq"), P(), P("chan")),
        out_specs=P(None, ("chan", "freq"), None, None),
        check_vma=False,
    )
```

```python
import functools
import math

import jax
import jax.numpy as jnp
import numpy as np
from jax import lax
from jax.experimental import pallas as pl
from jax.experimental.pallas import tpu as pltpu
from jax.sharding import PartitionSpec as P

W = 64
F = 512
HALF_LAG = 192
LAGS = 384
CH = 32
BINS = 128
KW = 2 * W
GROUPS = 4
OWN = CH // GROUPS
QUAD = 4
EPS = 1e-06
STEP = BINS + 8
PITCH = 2 * CH + 8
SMALL = pl.CostEstimate(flops=1, bytes_accessed=1, transcendentals=0)


def whiten_kernel(offsets_ref, alive_ref, x_ref, out_ref, rest_ref, turned):
    rest_ref[0] = offsets_ref[0] + offsets_ref[1] + offsets_ref[2]

    def one_channel(c, carry):
        re = x_ref[0, c].astype(jnp.float32)
        im = x_ref[1, c].astype(jnp.float32)
        energy = jnp.mean(re * re + im * im, axis=1, keepdims=True)
        scale = alive_ref[c].astype(jnp.float32) / jnp.sqrt(energy + EPS)
        both = jnp.concatenate([re * scale, im * scale], axis=0)
        turned[pl.ds(pl.multiple_of(c * STEP, 8), BINS), :] = both.T
        return carry

    lax.fori_loop(0, CH, one_channel, 0, unroll=8)

    def one_bin(f, carry):
        rows = turned[pl.ds(f, CH, stride=STEP), :]
        out_ref[f] = rows.astype(jnp.bfloat16)
        return carry

    lax.fori_loop(0, BINS, one_bin, 0, unroll=16)


def whiten(spectra, offsets, alive):
    return pl.pallas_call(
        whiten_kernel,
        out_shape=[jax.ShapeDtypeStruct((BINS, CH, KW), jnp.bfloat16), jax.ShapeDtypeStruct((1,), jnp.int32)],
        in_specs=[pl.BlockSpec(memory_space=pltpu.SMEM)] * 2 + [pl.BlockSpec(memory_space=pltpu.VMEM)],
        out_specs=[pl.BlockSpec(memory_space=pltpu.VMEM), pl.BlockSpec(memory_space=pltpu.SMEM)],
        scratch_shapes=[pltpu.VMEM((CH * STEP, KW), jnp.float32)],
        compiler_params=pltpu.CompilerParams(vmem_limit_bytes=62 << 20),
        cost_estimate=SMALL,
    )(offsets, alive, spectra)


def rotate_kernel(own_ref, out_ref):
    lane = lax.broadcasted_iota(jnp.int32, (CH, KW), 1)

    def one_bin(f, carry):
        rows = own_ref[f]
        out_ref[f, 0:CH, :] = rows
        other = pltpu.roll(rows.astype(jnp.float32), W, 1)
        out_ref[f, CH : 2 * CH, :] = jnp.where(lane < W, other, -other).astype(jnp.bfloat16)
        return carry

    lax.fori_loop(0, BINS, one_bin, 0, unroll=8)


def rotate(own):
    return pl.pallas_call(
        rotate_kernel,
        out_shape=jax.ShapeDtypeStruct((BINS, 2 * CH, KW), jnp.bfloat16),
        in_specs=[pl.BlockSpec(memory_space=pltpu.VMEM)],
        out_specs=pl.BlockSpec(memory_space=pltpu.VMEM),
        compiler_params=pltpu.CompilerParams(vmem_limit_bytes=24 << 20),
        cost_estimate=SMALL,
    )(own)


def cross_kernel(layout, place_ref, own_ref, *rest):
    pieces, outs, scratch = rest[: len(rest) - 1 - len(layout)], rest[len(rest) - 1 - len(layout) : -1], rest[-1]
    group_refs = {}
    for out_ref, held in zip(outs, layout):
        for n, k in enumerate(held):
            group_refs[k] = out_ref.at[n]
    place = place_ref[0]
    first = 0
    for piece_ref in pieces:
        bins = piece_ref.shape[0]

        def one_bin(f, carry, first=first, piece_ref=piece_ref):
            here = pl.multiple_of((first + f) * PITCH, 8)
            scratch[pl.ds(here, 2 * CH), 0:CH] = lax.dot_general(
                own_ref[first + f], piece_ref[f], (((1,), (1,)), ((), ())), preferred_element_type=jnp.float32
            )
            return carry

        lax.fori_loop(0, bins, one_bin, 0, unroll=max(n for n in range(1, 33) if bins % n == 0))
        first += bins
    lane = lax.broadcasted_iota(jnp.int32, (BINS, KW), 1)
    for k in range(GROUPS):
        group = lax.bitwise_xor(place, k)

        def one_part(j, carry, k=k, group=group):
            for quad in range(OWN // QUAD):
                row = j * CH + group * OWN + quad * QUAD
                packed = scratch[pl.ds(row, BINS, stride=PITCH), :]
                for i in range(1, QUAD):
                    piece = scratch[pl.ds(row + i, BINS, stride=PITCH), :]
                    packed = jnp.where(lane >= CH * i, pltpu.roll(piece, CH * i, 1), packed)
                here = pl.ds(pl.multiple_of(j * BINS, BINS), BINS)
                group_refs[k][here, quad * QUAD * CH : (quad + 1) * QUAD * CH] = packed.astype(jnp.bfloat16)
            return carry

        lax.fori_loop(0, 2, one_part, 0)


def cross(place, own, pieces, layout):
    outs = [jax.ShapeDtypeStruct((len(held), 2 * BINS, OWN * CH), jnp.bfloat16) for held in layout]
    return pl.pallas_call(
        functools.partial(cross_kernel, layout),
        out_shape=outs,
        in_specs=[pl.BlockSpec(memory_space=pltpu.SMEM)] + [pl.BlockSpec(memory_space=pltpu.VMEM)] * (1 + len(pieces)),
        out_specs=[pl.BlockSpec(memory_space=pltpu.VMEM)] * len(outs),
        scratch_shapes=[pltpu.VMEM((BINS * PITCH, KW), jnp.float32)],
        compiler_params=pltpu.CompilerParams(vmem_limit_bytes=24 << 20),
        cost_estimate=SMALL,
    )(place, own, *pieces)


@functools.cache
def lag_tables():
    bins = np.arange(F)[:, None]
    lags = np.arange(LAGS)[None, :] - HALF_LAG
    angle = np.mod(bins * lags, 2 * F) * (math.pi / F)
    factor = 1.0 / math.sqrt(W * F)
    table = np.stack([np.cos(angle), -np.sin(angle)]) * factor
    table = table.reshape(2, GROUPS, BINS, LAGS).transpose(1, 3, 0, 2).reshape(GROUPS, LAGS, 2 * BINS)
    high = table.astype(jnp.bfloat16)
    low = (table - high.astype(np.float64)).astype(jnp.bfloat16)
    return high, low


def lags_kernel(counts, offsets_ref, place_ref, high_ref, low_ref, *rest):
    out_ref = rest[-1]
    place = place_ref[0]

    def one_item(parts):
        blocks = [part.at[n] for part in parts for n in range(part.shape[0])]
        total = jnp.zeros((LAGS, OWN * CH), jnp.float32)
        for k in range(GROUPS):
            source = lax.bitwise_xor(place, k)
            terms = blocks[k][...]
            total += jnp.dot(high_ref[source], terms, preferred_element_type=jnp.float32)
            total += jnp.dot(low_ref[source], terms, preferred_element_type=jnp.float32)
        out_ref[0] = total.T

    first = 0
    for item, count in enumerate(counts):
        pl.when(pl.program_id(0) == item)(functools.partial(one_item, rest[first : first + count]))
        first += count


def lags(offsets, place, tables, items):
    def block_of(step, offsets_ref, place_ref):
        one = jnp.where(offsets_ref[0] == 1, 0, jnp.where(offsets_ref[1] == 1, 1, 2))
        far = jnp.where(offsets_ref[0] == 32, 0, jnp.where(offsets_ref[1] == 32, 1, 2))
        return jnp.where(step == 0, one, jnp.where(step == 1, far, 3 - one - far)), 0, 0

    counts = [len(parts) for parts in items]
    return pl.pallas_call(
        functools.partial(lags_kernel, counts),
        out_shape=jax.ShapeDtypeStruct((len(items), OWN * CH, LAGS), jnp.float32),
        grid_spec=pltpu.PrefetchScalarGridSpec(
            num_scalar_prefetch=2,
            grid=(len(items),),
            in_specs=[pl.BlockSpec(memory_space=pltpu.VMEM)] * (2 + sum(counts)),
            out_specs=pl.BlockSpec((1, OWN * CH, LAGS), block_of),
        ),
        compiler_params=pltpu.CompilerParams(vmem_limit_bytes=24 << 20),
        cost_estimate=SMALL,
    )(offsets, place, *tables, *[part for parts in items for part in parts])


def swap(block, k):
    return lax.ppermute(block, "freq", [(i, i ^ k) for i in range(GROUPS)])


def walk(block, before, after):
    count = lax.axis_size("chan")
    route = [(before(b) % count, after(b) % count) for b in range(count)]
    return lax.ppermute(block, "chan", route)


def home(b):
    return b


def ahead(distance):
    return lambda b: b + distance


def local(spectra, offsets, alive):
    half = lax.axis_size("chan") // 2
    place = lax.axis_index("freq").astype(jnp.int32).reshape(1)
    layout = [(k,) for k in range(GROUPS)]
    tables = [jnp.asarray(t) for t in lag_tables()]

    def spread(groups):
        return [groups[0]] + [swap(groups[k], k) for k in (1, 2, 3)]

    own, total = whiten(spectra, offsets, alive)
    next_one = walk(own, home, ahead(1))
    far_one = walk(own, home, ahead(half))
    branches = [functools.partial(walk, before=home, after=ahead(d)) for d in range(2, half)]
    other = lax.switch(total[0] - (1 + half + 2), branches, own)
    both = rotate(own)
    items = [spread(cross(place, both, [partner], layout)) for partner in (next_one, far_one, other)]
    return lags(offsets, place, tables, items).reshape(3, OWN, CH, LAGS)


def solution(mesh):
    return jax.shard_map(
        local,
        mesh=mesh,
        in_specs=(P(None, "chan", None, "freq"), P(), P("chan")),
        out_specs=P(None, ("chan", "freq"), None, None),
        check_vma=False,
    )
```

```python
import functools
import math

import jax
import jax.numpy as jnp
import numpy as np
from jax import lax
from jax.experimental import pallas as pl
from jax.experimental.pallas import tpu as pltpu
from jax.sharding import PartitionSpec as P

W = 64
F = 512
HALF_LAG = 192
LAGS = 384
CH = 32
BINS = 128
KW = 2 * W
GROUPS = 4
OWN = CH // GROUPS
QUAD = 4
EPS = 1e-06
STEP = BINS + 8
PITCH = 2 * CH + 8
SMALL = pl.CostEstimate(flops=1, bytes_accessed=1, transcendentals=0)


def whiten_kernel(offsets_ref, alive_ref, x_ref, out_ref, rest_ref, turned):
    rest_ref[0] = offsets_ref[0] + offsets_ref[1] + offsets_ref[2]

    def one_channel(c, carry):
        re = x_ref[0, c].astype(jnp.float32)
        im = x_ref[1, c].astype(jnp.float32)
        energy = jnp.mean(re * re + im * im, axis=1, keepdims=True)
        scale = alive_ref[c].astype(jnp.float32) / jnp.sqrt(energy + EPS)
        both = jnp.concatenate([re * scale, im * scale], axis=0)
        turned[pl.ds(pl.multiple_of(c * STEP, 8), BINS), :] = both.T
        return carry

    lax.fori_loop(0, CH, one_channel, 0, unroll=8)

    def one_bin(f, carry):
        rows = turned[pl.ds(f, CH, stride=STEP), :]
        out_ref[f] = rows.astype(jnp.bfloat16)
        return carry

    lax.fori_loop(0, BINS, one_bin, 0, unroll=16)


def whiten(spectra, offsets, alive):
    return pl.pallas_call(
        whiten_kernel,
        out_shape=[jax.ShapeDtypeStruct((BINS, CH, KW), jnp.bfloat16), jax.ShapeDtypeStruct((1,), jnp.int32)],
        in_specs=[pl.BlockSpec(memory_space=pltpu.SMEM)] * 2 + [pl.BlockSpec(memory_space=pltpu.VMEM)],
        out_specs=[pl.BlockSpec(memory_space=pltpu.VMEM), pl.BlockSpec(memory_space=pltpu.SMEM)],
        scratch_shapes=[pltpu.VMEM((CH * STEP, KW), jnp.float32)],
        compiler_params=pltpu.CompilerParams(vmem_limit_bytes=62 << 20),
        cost_estimate=SMALL,
    )(offsets, alive, spectra)


def rotate_kernel(own_ref, out_ref):
    lane = lax.broadcasted_iota(jnp.int32, (CH, KW), 1)

    def one_bin(f, carry):
        rows = own_ref[f]
        out_ref[f, 0:CH, :] = rows
        other = pltpu.roll(rows.astype(jnp.float32), W, 1)
        out_ref[f, CH : 2 * CH, :] = jnp.where(lane < W, other, -other).astype(jnp.bfloat16)
        return carry

    lax.fori_loop(0, BINS, one_bin, 0, unroll=8)


def rotate(own):
    return pl.pallas_call(
        rotate_kernel,
        out_shape=jax.ShapeDtypeStruct((BINS, 2 * CH, KW), jnp.bfloat16),
        in_specs=[pl.BlockSpec(memory_space=pltpu.VMEM)],
        out_specs=pl.BlockSpec(memory_space=pltpu.VMEM),
        compiler_params=pltpu.CompilerParams(vmem_limit_bytes=24 << 20),
        cost_estimate=SMALL,
    )(own)


def cross_kernel(layout, place_ref, own_ref, *rest):
    pieces, outs, scratch = rest[: len(rest) - 1 - len(layout)], rest[len(rest) - 1 - len(layout) : -1], rest[-1]
    group_refs = {}
    for out_ref, held in zip(outs, layout):
        for n, k in enumerate(held):
            group_refs[k] = out_ref.at[n]
    place = place_ref[0]
    first = 0
    for piece_ref in pieces:
        bins = piece_ref.shape[0]

        def one_bin(f, carry, first=first, piece_ref=piece_ref):
            here = pl.multiple_of((first + f) * PITCH, 8)
            scratch[pl.ds(here, 2 * CH), 0:CH] = lax.dot_general(
                own_ref[first + f], piece_ref[f], (((1,), (1,)), ((), ())), preferred_element_type=jnp.float32
            )
            return carry

        lax.fori_loop(0, bins, one_bin, 0, unroll=max(n for n in range(1, 33) if bins % n == 0))
        first += bins
    lane = lax.broadcasted_iota(jnp.int32, (BINS, KW), 1)
    for k in range(GROUPS):
        group = lax.bitwise_xor(place, k)

        def one_part(j, carry, k=k, group=group):
            for quad in range(OWN // QUAD):
                row = j * CH + group * OWN + quad * QUAD
                packed = scratch[pl.ds(row, BINS, stride=PITCH), :]
                for i in range(1, QUAD):
                    piece = scratch[pl.ds(row + i, BINS, stride=PITCH), :]
                    packed = jnp.where(lane >= CH * i, pltpu.roll(piece, CH * i, 1), packed)
                here = pl.ds(pl.multiple_of(j * BINS, BINS), BINS)
                group_refs[k][here, quad * QUAD * CH : (quad + 1) * QUAD * CH] = packed.astype(jnp.bfloat16)
            return carry

        lax.fori_loop(0, 2, one_part, 0)


def cross(place, own, pieces, layout):
    outs = [jax.ShapeDtypeStruct((len(held), 2 * BINS, OWN * CH), jnp.bfloat16) for held in layout]
    return pl.pallas_call(
        functools.partial(cross_kernel, layout),
        out_shape=outs,
        in_specs=[pl.BlockSpec(memory_space=pltpu.SMEM)] + [pl.BlockSpec(memory_space=pltpu.VMEM)] * (1 + len(pieces)),
        out_specs=[pl.BlockSpec(memory_space=pltpu.VMEM)] * len(outs),
        scratch_shapes=[pltpu.VMEM((BINS * PITCH, KW), jnp.float32)],
        compiler_params=pltpu.CompilerParams(vmem_limit_bytes=24 << 20),
        cost_estimate=SMALL,
    )(place, own, *pieces)


@functools.cache
def lag_tables():
    bins = np.arange(F)[:, None]
    lags = np.arange(LAGS)[None, :] - HALF_LAG
    angle = np.mod(bins * lags, 2 * F) * (math.pi / F)
    factor = 1.0 / math.sqrt(W * F)
    table = np.stack([np.cos(angle), -np.sin(angle)]) * factor
    table = table.reshape(2, GROUPS, BINS, LAGS).transpose(1, 3, 0, 2).reshape(GROUPS, LAGS, 2 * BINS)
    high = table.astype(jnp.bfloat16)
    low = (table - high.astype(np.float64)).astype(jnp.bfloat16)
    return high, low


def lags_kernel(counts, offsets_ref, place_ref, high_ref, low_ref, *rest):
    out_ref = rest[-1]
    place = place_ref[0]

    def one_item(parts):
        blocks = [part.at[n] for part in parts for n in range(part.shape[0])]
        total = jnp.zeros((LAGS, OWN * CH), jnp.float32)
        for k in range(GROUPS):
            source = lax.bitwise_xor(place, k)
            terms = blocks[k][...]
            total += jnp.dot(high_ref[source], terms, preferred_element_type=jnp.float32)
            total += jnp.dot(low_ref[source], terms, preferred_element_type=jnp.float32)
        out_ref[0] = total.T

    first = 0
    for item, count in enumerate(counts):
        pl.when(pl.program_id(0) == item)(functools.partial(one_item, rest[first : first + count]))
        first += count


def lags(offsets, place, tables, items):
    def block_of(step, offsets_ref, place_ref):
        one = jnp.where(offsets_ref[0] == 1, 0, jnp.where(offsets_ref[1] == 1, 1, 2))
        far = jnp.where(offsets_ref[0] == 32, 0, jnp.where(offsets_ref[1] == 32, 1, 2))
        return jnp.where(step == 0, one, jnp.where(step == 1, far, 3 - one - far)), 0, 0

    counts = [len(parts) for parts in items]
    return pl.pallas_call(
        functools.partial(lags_kernel, counts),
        out_shape=jax.ShapeDtypeStruct((len(items), OWN * CH, LAGS), jnp.float32),
        grid_spec=pltpu.PrefetchScalarGridSpec(
            num_scalar_prefetch=2,
            grid=(len(items),),
            in_specs=[pl.BlockSpec(memory_space=pltpu.VMEM)] * (2 + sum(counts)),
            out_specs=pl.BlockSpec((1, OWN * CH, LAGS), block_of),
        ),
        compiler_params=pltpu.CompilerParams(vmem_limit_bytes=24 << 20),
        cost_estimate=SMALL,
    )(offsets, place, *tables, *[part for parts in items for part in parts])


def swap(block, k):
    return lax.ppermute(block, "freq", [(i, i ^ k) for i in range(GROUPS)])


def walk(block, before, after):
    count = lax.axis_size("chan")
    route = [(before(b) % count, after(b) % count) for b in range(count)]
    return lax.ppermute(block, "chan", route)


def home(b):
    return b


def ahead(distance):
    return lambda b: b + distance


def local(spectra, offsets, alive):
    half = lax.axis_size("chan") // 2
    place = lax.axis_index("freq").astype(jnp.int32).reshape(1)
    layout = [(k,) for k in range(GROUPS)]
    tables = [jnp.asarray(t) for t in lag_tables()]

    def spread(groups):
        return [groups[0]] + [swap(groups[k], k) for k in (1, 2, 3)]

    own, total = whiten(spectra, offsets, alive)
    next_one = walk(own, home, ahead(1))
    far_one = walk(own, home, ahead(half))
    branches = [functools.partial(walk, before=home, after=ahead(d)) for d in range(2, half)]
    other = lax.switch(total[0] - (1 + half + 2), branches, own)
    both = rotate(own)
    near = cross(place, both, [next_one], layout)
    near, other = lax.optimization_barrier((near, other))
    last = cross(place, both, [other], layout)
    last, far_one = lax.optimization_barrier((last, far_one))
    far = cross(place, both, [far_one], layout)
    return lags(offsets, place, tables, [spread(near), spread(far), spread(last)]).reshape(3, OWN, CH, LAGS)


def solution(mesh):
    return jax.shard_map(
        local,
        mesh=mesh,
        in_specs=(P(None, "chan", None, "freq"), P(), P("chan")),
        out_specs=P(None, ("chan", "freq"), None, None),
        check_vma=False,
    )
```

```python
import functools
import math

import jax
import jax.numpy as jnp
import numpy as np
from jax import lax
from jax.experimental import pallas as pl
from jax.experimental.pallas import tpu as pltpu
from jax.sharding import PartitionSpec as P

W = 64
F = 512
HALF_LAG = 192
LAGS = 384
CH = 32
BINS = 128
KW = 2 * W
GROUPS = 4
OWN = CH // GROUPS
QUAD = 4
EPS = 1e-06
STEP = BINS + 8
PITCH = 2 * CH + 8
SMALL = pl.CostEstimate(flops=1, bytes_accessed=1, transcendentals=0)


def whiten_kernel(offsets_ref, alive_ref, x_ref, out_ref, rest_ref, turned):
    rest_ref[0] = offsets_ref[0] + offsets_ref[1] + offsets_ref[2]

    def one_channel(c, carry):
        re = x_ref[0, c].astype(jnp.float32)
        im = x_ref[1, c].astype(jnp.float32)
        energy = jnp.mean(re * re + im * im, axis=1, keepdims=True)
        scale = alive_ref[c].astype(jnp.float32) / jnp.sqrt(energy + EPS)
        both = jnp.concatenate([re * scale, im * scale], axis=0)
        turned[pl.ds(pl.multiple_of(c * STEP, 8), BINS), :] = both.T
        return carry

    lax.fori_loop(0, CH, one_channel, 0, unroll=8)

    def one_bin(f, carry):
        rows = turned[pl.ds(f, CH, stride=STEP), :]
        out_ref[f] = rows.astype(jnp.bfloat16)
        return carry

    lax.fori_loop(0, BINS, one_bin, 0, unroll=16)


def whiten(spectra, offsets, alive):
    return pl.pallas_call(
        whiten_kernel,
        out_shape=[jax.ShapeDtypeStruct((BINS, CH, KW), jnp.bfloat16), jax.ShapeDtypeStruct((1,), jnp.int32)],
        in_specs=[pl.BlockSpec(memory_space=pltpu.SMEM)] * 2 + [pl.BlockSpec(memory_space=pltpu.VMEM)],
        out_specs=[pl.BlockSpec(memory_space=pltpu.VMEM), pl.BlockSpec(memory_space=pltpu.SMEM)],
        scratch_shapes=[pltpu.VMEM((CH * STEP, KW), jnp.float32)],
        compiler_params=pltpu.CompilerParams(vmem_limit_bytes=62 << 20),
        cost_estimate=SMALL,
    )(offsets, alive, spectra)


def rotate_kernel(own_ref, out_ref):
    lane = lax.broadcasted_iota(jnp.int32, (CH, KW), 1)

    def one_bin(f, carry):
        rows = own_ref[f]
        out_ref[f, 0:CH, :] = rows
        other = pltpu.roll(rows.astype(jnp.float32), W, 1)
        out_ref[f, CH : 2 * CH, :] = jnp.where(lane < W, other, -other).astype(jnp.bfloat16)
        return carry

    lax.fori_loop(0, BINS, one_bin, 0, unroll=8)


def rotate(own):
    return pl.pallas_call(
        rotate_kernel,
        out_shape=jax.ShapeDtypeStruct((BINS, 2 * CH, KW), jnp.bfloat16),
        in_specs=[pl.BlockSpec(memory_space=pltpu.VMEM)],
        out_specs=pl.BlockSpec(memory_space=pltpu.VMEM),
        compiler_params=pltpu.CompilerParams(vmem_limit_bytes=24 << 20),
        cost_estimate=SMALL,
    )(own)


def cross_kernel(layout, place_ref, own_ref, *rest):
    pieces, outs, scratch = rest[: len(rest) - 1 - len(layout)], rest[len(rest) - 1 - len(layout) : -1], rest[-1]
    group_refs = {}
    for out_ref, held in zip(outs, layout):
        for n, k in enumerate(held):
            group_refs[k] = out_ref.at[n]
    place = place_ref[0]
    first = 0
    for piece_ref in pieces:
        bins = piece_ref.shape[0]

        def one_bin(f, carry, first=first, piece_ref=piece_ref):
            here = pl.multiple_of((first + f) * PITCH, 8)
            scratch[pl.ds(here, 2 * CH), 0:CH] = lax.dot_general(
                own_ref[first + f], piece_ref[f], (((1,), (1,)), ((), ())), preferred_element_type=jnp.float32
            )
            return carry

        lax.fori_loop(0, bins, one_bin, 0, unroll=max(n for n in range(1, 33) if bins % n == 0))
        first += bins
    lane = lax.broadcasted_iota(jnp.int32, (BINS, KW), 1)
    for k in range(GROUPS):
        group = lax.bitwise_xor(place, k)

        def one_part(j, carry, k=k, group=group):
            for quad in range(OWN // QUAD):
                row = j * CH + group * OWN + quad * QUAD
                packed = scratch[pl.ds(row, BINS, stride=PITCH), :]
                for i in range(1, QUAD):
                    piece = scratch[pl.ds(row + i, BINS, stride=PITCH), :]
                    packed = jnp.where(lane >= CH * i, pltpu.roll(piece, CH * i, 1), packed)
                here = pl.ds(pl.multiple_of(j * BINS, BINS), BINS)
                group_refs[k][here, quad * QUAD * CH : (quad + 1) * QUAD * CH] = packed.astype(jnp.bfloat16)
            return carry

        lax.fori_loop(0, 2, one_part, 0)


def cross(place, own, pieces, layout):
    outs = [jax.ShapeDtypeStruct((len(held), 2 * BINS, OWN * CH), jnp.bfloat16) for held in layout]
    return pl.pallas_call(
        functools.partial(cross_kernel, layout),
        out_shape=outs,
        in_specs=[pl.BlockSpec(memory_space=pltpu.SMEM)] + [pl.BlockSpec(memory_space=pltpu.VMEM)] * (1 + len(pieces)),
        out_specs=[pl.BlockSpec(memory_space=pltpu.VMEM)] * len(outs),
        scratch_shapes=[pltpu.VMEM((BINS * PITCH, KW), jnp.float32)],
        compiler_params=pltpu.CompilerParams(vmem_limit_bytes=24 << 20),
        cost_estimate=SMALL,
    )(place, own, *pieces)


@functools.cache
def lag_tables():
    bins = np.arange(F)[:, None]
    lags = np.arange(LAGS)[None, :] - HALF_LAG
    angle = np.mod(bins * lags, 2 * F) * (math.pi / F)
    factor = 1.0 / math.sqrt(W * F)
    table = np.stack([np.cos(angle), -np.sin(angle)]) * factor
    table = table.reshape(2, GROUPS, BINS, LAGS).transpose(1, 3, 0, 2).reshape(GROUPS, LAGS, 2 * BINS)
    high = table.astype(jnp.bfloat16)
    low = (table - high.astype(np.float64)).astype(jnp.bfloat16)
    return high, low


def lags_kernel(counts, offsets_ref, place_ref, high_ref, low_ref, *rest):
    out_ref = rest[-1]
    place = place_ref[0]

    def one_item(parts):
        blocks = [part.at[n] for part in parts for n in range(part.shape[0])]
        total = jnp.zeros((LAGS, OWN * CH), jnp.float32)
        for k in range(GROUPS):
            source = lax.bitwise_xor(place, k)
            terms = blocks[k][...]
            total += jnp.dot(high_ref[source], terms, preferred_element_type=jnp.float32)
            total += jnp.dot(low_ref[source], terms, preferred_element_type=jnp.float32)
        out_ref[0] = total.T

    first = 0
    for item, count in enumerate(counts):
        pl.when(pl.program_id(0) == item)(functools.partial(one_item, rest[first : first + count]))
        first += count


def lags(offsets, place, tables, items):
    def block_of(step, offsets_ref, place_ref):
        one = jnp.where(offsets_ref[0] == 1, 0, jnp.where(offsets_ref[1] == 1, 1, 2))
        far = jnp.where(offsets_ref[0] == 32, 0, jnp.where(offsets_ref[1] == 32, 1, 2))
        return jnp.where(step == 0, one, jnp.where(step == 1, far, 3 - one - far)), 0, 0

    counts = [len(parts) for parts in items]
    return pl.pallas_call(
        functools.partial(lags_kernel, counts),
        out_shape=jax.ShapeDtypeStruct((len(items), OWN * CH, LAGS), jnp.float32),
        grid_spec=pltpu.PrefetchScalarGridSpec(
            num_scalar_prefetch=2,
            grid=(len(items),),
            in_specs=[pl.BlockSpec(memory_space=pltpu.VMEM)] * (2 + sum(counts)),
            out_specs=pl.BlockSpec((1, OWN * CH, LAGS), block_of),
        ),
        compiler_params=pltpu.CompilerParams(vmem_limit_bytes=24 << 20),
        cost_estimate=SMALL,
    )(offsets, place, *tables, *[part for parts in items for part in parts])


def swap(block, k):
    return lax.ppermute(block, "freq", [(i, i ^ k) for i in range(GROUPS)])


def walk(block, before, after):
    count = lax.axis_size("chan")
    route = [(before(b) % count, after(b) % count) for b in range(count)]
    return lax.ppermute(block, "chan", route)


def home(b):
    return b


def ahead(distance):
    return lambda b: b + distance


def local(spectra, offsets, alive):
    half = lax.axis_size("chan") // 2
    place = lax.axis_index("freq").astype(jnp.int32).reshape(1)
    layout = [(k,) for k in range(GROUPS)]
    tables = [jnp.asarray(t) for t in lag_tables()]

    def spread(groups):
        return [groups[0]] + [swap(groups[k], k) for k in (1, 2, 3)]

    own, total = whiten(spectra, offsets, alive)
    next_one = walk(own, home, ahead(1))
    far_one = walk(own, home, ahead(half))
    branches = [functools.partial(walk, before=home, after=ahead(d)) for d in range(2, half)]
    other = lax.switch(total[0] - (1 + half + 2), branches, own)
    both = rotate(own)
    near = cross(place, both, [next_one], layout)
    near, far_one = lax.optimization_barrier((near, far_one))
    far, last = cross(place, both, [far_one], layout), cross(place, both, [other], layout)
    return lags(offsets, place, tables, [spread(near), spread(far), spread(last)]).reshape(3, OWN, CH, LAGS)


def solution(mesh):
    return jax.shard_map(
        local,
        mesh=mesh,
        in_specs=(P(None, "chan", None, "freq"), P(), P("chan")),
        out_specs=P(None, ("chan", "freq"), None, None),
        check_vma=False,
    )
```
